32 devices in a mesh: rep: 4 (over z), fsdp: 8 (over y, x, core).
Axes of the slice: x: 2, y: 2, z: 4, core: 2. Of those that a mesh axis runs over, the one named last changes fastest.
Arguments:
- grads: bfloat16 [4, 1024, 16384], P('rep', 'fsdp')
- moments: float32 [1024, 16384], P('fsdp', 'rep'), may hold values from 0.05 to 2
- factors: float32 [4, 8, 1024, 1024], P('rep', 'fsdp'), as said below
- roots: bfloat16 [4, 8, 1024, 1024], P('rep', 'fsdp'), as said below
- refresh: int32 [8], replicated, may hold values from 0 to 31, as said below
- owner: int32 [1, 16], replicated, may hold values from 0 to 3, as said below
Outputs:
- update: bfloat16 [1024, 16384], P('fsdp')
- new_moments: float32 [1024, 16384], P('fsdp', 'rep')
- new_factors: float32 [4, 8, 1024, 1024], P('rep', 'fsdp')
- new_roots: bfloat16 [4, 8, 1024, 1024], P('rep', 'fsdp')
The draws below stay inside these ranges and needn't reach their ends.
Inputs may be any that keep to these rules, and one draw needn't show every extreme that they name: `refresh`: 8 distinct factor ids below 32; no two of them are held at the same fsdp index. `owner`: every band gives exactly 4 of its column blocks to each group. `factors`: each matrix is symmetric and positive definite. `roots`: each matrix is symmetric.
All inputs are finite; a program needn't handle non-finite values.
Results may differ from the reference program's by a relative error of at most 0.015.
Values may be sent and summed in bfloat16 or wider, within the bound.
A program may use at most 128 MiB of HBM per device.

```python
import math
import jax
import jax.numpy as jnp
from jax import lax

ROWS = 128
BS = 1024
D = 1024
FF = 16384
SUB = 128
NCOLB = 16
BANDS = 1
NEWTON = 3
REFRESH = 8
N_REP = 4
N_FSDP = 8


def owner_table(key):
    band_keys = jax.random.split(key, BANDS)
    shuffled = jax.vmap(lambda band_key: jax.random.permutation(band_key, NCOLB))(band_keys)
    return (shuffled // (NCOLB // N_REP)).astype(jnp.int32)


def draw_owner(key, part):
    return owner_table(key)


def draw_refresh(key, part):
    owner_map = owner_table(key)
    key = jax.random.fold_in(key, 11)
    key_columns, key_groups = jax.random.split(key)
    band_span = BS // ROWS
    chosen_fsdp = jax.random.permutation(key_columns, N_FSDP)[:REFRESH]
    chosen_group = jax.random.randint(key_groups, (REFRESH,), 0, N_REP)
    band_index = chosen_fsdp // band_span
    local_index = chosen_fsdp % band_span
    col_range = jnp.arange(NCOLB, dtype=jnp.int32)
    col_order = jnp.argsort(owner_map * NCOLB + col_range[None, :], axis=1).astype(jnp.int32)
    position = chosen_group * (NCOLB // N_REP) + local_index // 2
    column_block = col_order[band_index, position]
    return (2 * (band_index * NCOLB + column_block) + local_index % 2).astype(jnp.int32)


def draw_grads(key, part):
    key = jax.random.fold_in(key, 3)
    key_own = jax.random.fold_in(key, 1)
    key_rows = jax.random.fold_in(key, 2)
    key_cols = jax.random.fold_in(key, 3)
    own_noise = jax.random.normal(key_own, (N_REP, D, FF), jnp.float32)
    noise_field = own_noise
    lowest, highest = (0.3, 3.0)
    row_scale = jnp.exp(jax.random.uniform(key_rows, (D,), jnp.float32, math.log(lowest), math.log(highest)))
    rising = 3.0 ** (jnp.arange(D).astype(jnp.float32) / D)
    col_scale = jnp.exp(jax.random.uniform(key_cols, (FF,), jnp.float32, math.log(lowest), math.log(highest)))
    return (noise_field * (row_scale * rising)[None, :, None] * col_scale[None, None, :]).astype(jnp.bfloat16)


def draw_factors(key, part):
    key = jax.random.fold_in(key, 5)
    key_base = jax.random.fold_in(key, 0)
    slot_total = N_REP * N_FSDP
    base_matrix = jax.random.normal(key_base, (slot_total, BS, BS), jnp.float32)
    gram_matrix = jnp.einsum('sij,skj->sik', base_matrix, base_matrix, precision=jax.lax.Precision.HIGHEST)
    identity = jnp.eye(BS, dtype=jnp.float32)
    value_all = 0.5 * gram_matrix + 0.05 * BS * identity[None, :, :]
    return value_all.reshape(N_REP, N_FSDP, BS, BS)


def draw_roots(key, part):
    key = jax.random.fold_in(key, 7)
    slot_total = N_REP * N_FSDP
    noise_field = jax.random.normal(key, (slot_total, BS, BS), jnp.float32)
    symmetric = (noise_field + jnp.swapaxes(noise_field, 1, 2)) * (0.25 / math.sqrt(BS))
    identity = jnp.eye(BS, dtype=jnp.float32)
    value_all = identity[None, :, :] + symmetric
    return value_all.reshape(N_REP, N_FSDP, BS, BS).astype(jnp.bfloat16)


def shard_levels(key, extent, shards, low, high):
    factor_of = 1.0
    for dim, blocks in shards:
        steps = jax.random.uniform(jax.random.fold_in(jax.random.fold_in(key, 6), dim), (blocks,), jnp.float32, low / len(shards), high / len(shards))
        factor_of = factor_of * jnp.repeat(jnp.exp(steps), extent[dim] // blocks).reshape((-1,) + (1,) * (len(extent) - 1 - dim))
    return factor_of


def setup_inputs(seed: int = 0) -> dict:
    arg_keys = jax.random.split(jax.random.key(seed), 7)
    grads = draw_grads(jax.random.fold_in(arg_keys[6], 71), 0)
    moments = jnp.clip(jnp.exp(math.log(2.0) - 3.6888794 * jax.random.uniform(arg_keys[1], (D, FF), jnp.float32) ** shard_levels(arg_keys[1], (D, FF), ((0, 8), (1, 4)), -0.2, 0.2)), 0.05, 2.0)
    factors = draw_factors(jax.random.fold_in(arg_keys[6], 71), 0)
    roots = draw_roots(jax.random.fold_in(arg_keys[6], 71), 0)
    refresh = draw_refresh(jax.random.fold_in(arg_keys[6], 71), 0)
    owner = draw_owner(jax.random.fold_in(arg_keys[6], 71), 0)
    return dict(grads=grads, moments=moments, factors=factors, roots=roots, refresh=refresh, owner=owner)


BETA_FACTOR = 0.9
BETA_MOMENT = 0.95
EPS_ADAM = 1e-08
EPS_NORM = 1e-06

def newton_seed(factor):
    norm_value = jnp.sqrt(jnp.sum(factor * factor))
    state_now = (factor / norm_value).astype(jnp.bfloat16)
    first_scale = norm_value ** (-0.25)
    return (state_now, first_scale)

def newton_step_matrix(state_now, identity):
    return ((5.0 * identity - state_now.astype(jnp.float32)) * 0.25).astype(jnp.bfloat16)

def newton_whole(factor):
    identity = jnp.eye(factor.shape[0], dtype=jnp.float32)
    state_now, first_scale = newton_seed(factor)
    root_now = (first_scale * identity).astype(jnp.bfloat16)
    for iteration in range(NEWTON):
        step_mat = newton_step_matrix(state_now, identity)
        root_now = jnp.dot(root_now, step_mat, preferred_element_type=jnp.float32).astype(jnp.bfloat16)
        if iteration + 1 < NEWTON:
            square = jnp.dot(step_mat, step_mat, preferred_element_type=jnp.float32).astype(jnp.bfloat16)
            fourth = jnp.dot(square, square, preferred_element_type=jnp.float32).astype(jnp.bfloat16)
            state_now = jnp.dot(fourth, state_now, preferred_element_type=jnp.float32).astype(jnp.bfloat16)
    return root_now

def block_work(packed):
    grad_block, left_old, right_old, left_root, right_root = packed
    left_gram = jnp.dot(grad_block, grad_block.T, preferred_element_type=jnp.float32)
    right_gram = jnp.dot(grad_block.T, grad_block, preferred_element_type=jnp.float32)
    left_new = BETA_FACTOR * left_old + (1.0 - BETA_FACTOR) * left_gram
    right_new = BETA_FACTOR * right_old + (1.0 - BETA_FACTOR) * right_gram
    mixed_rows = jnp.dot(left_root, grad_block, preferred_element_type=jnp.float32).astype(jnp.bfloat16)
    product = jnp.dot(mixed_rows, right_root, preferred_element_type=jnp.float32)
    return (left_new, right_new, product)

def to_bands(matrix):
    return jnp.transpose(matrix.reshape(N_FSDP, BANDS, SUB, NCOLB, BS), (1, 0, 2, 3, 4)).reshape(BANDS, BS, NCOLB, BS)

def from_bands(matrix):
    return jnp.transpose(matrix.reshape(BANDS, N_FSDP, SUB, NCOLB, BS), (1, 0, 2, 3, 4)).reshape(D, FF)

def reference(grads, moments, factors, roots, refresh, owner):
    slot_count = NCOLB // N_REP
    band_span = BS // ROWS
    gradient = lax.optimization_barrier(jnp.sum(grads.astype(jnp.float32), axis=0)) / N_REP
    col_range = jnp.arange(NCOLB, dtype=jnp.int32)
    col_order = jnp.argsort(owner * NCOLB + col_range[None, :], axis=1).astype(jnp.int32)
    blocks = to_bands(gradient)
    owned_grad = jnp.take_along_axis(blocks, col_order[:, None, :, None], axis=2)
    moment_old = to_bands(moments)
    moment_new = BETA_MOMENT * moment_old + (1.0 - BETA_MOMENT) * owned_grad * owned_grad
    adam_dir = owned_grad / (jnp.sqrt(moment_new) + EPS_ADAM)
    adam_sq = lax.optimization_barrier(jnp.sum(adam_dir * adam_dir, axis=(1, 3))).reshape(BANDS, N_REP, slot_count)
    adam_sq = jnp.transpose(adam_sq, (1, 0, 2)).reshape(-1)
    grad_low = owned_grad.astype(jnp.bfloat16).reshape(BANDS, BS, N_REP, slot_count, BS)
    grad_low = jnp.transpose(grad_low, (2, 0, 3, 1, 4)).reshape(-1, BS, BS)
    old_factors = factors.reshape(N_REP * BANDS * slot_count, 2, BS, BS)
    old_roots = roots.reshape(N_REP * BANDS * slot_count, 2, BS, BS)
    left_new, right_new, product = lax.map(block_work, (grad_low, old_factors[:, 0], old_factors[:, 1], old_roots[:, 0], old_roots[:, 1]))
    product_sq = lax.optimization_barrier(jnp.sum(product * product, axis=(1, 2)))
    graft_scale = jnp.sqrt(adam_sq) * lax.rsqrt(product_sq + EPS_NORM)
    update_blocks = (product * graft_scale[:, None, None]).astype(jnp.bfloat16)
    update_owned = update_blocks.reshape(N_REP, BANDS, slot_count, BS, BS)
    update_owned = jnp.transpose(update_owned, (1, 3, 0, 2, 4)).reshape(BANDS, BS, NCOLB, BS)
    inverse = jnp.argsort(col_order, axis=1).astype(jnp.int32)
    update = from_bands(jnp.take_along_axis(update_owned, inverse[:, None, :, None], axis=2))
    new_factors = jnp.stack([left_new, right_new], axis=1).reshape(N_REP, N_FSDP, BS, BS)
    pair_ids = refresh // 2
    listed_band = (pair_ids // NCOLB).astype(jnp.int32)
    listed_col = (pair_ids % NCOLB).astype(jnp.int32)
    listed_rows = jnp.take(owner, listed_band, axis=0)
    listed_group = jnp.take_along_axis(listed_rows, listed_col[:, None], axis=1)[:, 0].astype(jnp.int32)
    listed_rank = lax.optimization_barrier(jnp.sum(((listed_rows == listed_group[:, None]) & (col_range[None, :] < listed_col[:, None])).astype(jnp.int32), axis=1))
    listed_fsdp = (listed_band * band_span + 2 * listed_rank + refresh % 2).astype(jnp.int32)
    chosen = new_factors[listed_group, listed_fsdp]
    fresh_roots = lax.map(newton_whole, chosen)
    new_roots = roots.at[listed_group, listed_fsdp].set(fresh_roots)
    return (update, from_bands(moment_new), new_factors, new_roots)
```

```python
import jax
import jax.numpy as jnp
from jax import lax
from jax.experimental import pallas as pl
from jax.experimental.pallas import tpu as pltpu
from jax.sharding import PartitionSpec as P

NEWTON = 3


BETA_FACTOR = 0.9
BETA_MOMENT = 0.95
EPS_ADAM = 1e-08
EPS_NORM = 1e-06


def from_partner(shard, axis, stride):
    return lax.ppermute(shard, axis, [(i, i ^ 1 << stride) for i in range(lax.axis_size(axis))])


def newton_seed(factor):
    norm_value = jnp.sqrt(jnp.sum(factor * factor))
    state_now = (factor / norm_value).astype(jnp.bfloat16)
    first_scale = norm_value ** (-0.25)
    return (state_now, first_scale)


def newton_step_matrix(state_now, identity):
    return ((5.0 * identity - state_now.astype(jnp.float32)) * 0.25).astype(jnp.bfloat16)


def newton_whole(factor):
    identity = jnp.eye(factor.shape[0], dtype=jnp.float32)
    state_now, first_scale = newton_seed(factor)
    root_now = (first_scale * identity).astype(jnp.bfloat16)
    for iteration in range(NEWTON):
        step_mat = newton_step_matrix(state_now, identity)
        root_now = jnp.dot(root_now, step_mat, preferred_element_type=jnp.float32).astype(
            jnp.bfloat16
        )
        if iteration + 1 < NEWTON:
            square = jnp.dot(step_mat, step_mat, preferred_element_type=jnp.float32).astype(
                jnp.bfloat16
            )
            fourth = jnp.dot(square, square, preferred_element_type=jnp.float32).astype(
                jnp.bfloat16
            )
            state_now = jnp.dot(fourth, state_now, preferred_element_type=jnp.float32).astype(
                jnp.bfloat16
            )
    return root_now


def copy_block(order_ref, in_ref, out_ref):
    out_ref[...] = in_ref[...].reshape(out_ref.shape)


def owner_order(rows, col_order, groups, band_count, sub_rows, block_size):
    per_group = col_order.shape[1] // groups
    pairs = band_count * per_group

    def source(i, order_ref):
        group, pair = i // pairs, i % pairs
        band, slot = pair // per_group, pair % per_group
        return band, order_ref[band * groups * per_group + group * per_group + slot]

    return pl.pallas_call(
        copy_block,
        grid_spec=pltpu.PrefetchScalarGridSpec(
            num_scalar_prefetch=1,
            grid=(groups * pairs,),
            in_specs=[pl.BlockSpec((sub_rows, block_size), source)],
            out_specs=pl.BlockSpec((1, sub_rows, block_size), lambda i, order_ref: (i, 0, 0)),
        ),
        out_shape=jax.ShapeDtypeStruct((groups * pairs, sub_rows, block_size), rows.dtype),
        name="owner_order",
    )(col_order.reshape(-1), rows)


def natural_order(pieces, col_order, groups, band_count, sub_rows, block_size):
    columns = col_order.shape[1]
    per_group = columns // groups
    pairs = band_count * per_group

    def target(i, order_ref):
        group, pair = i // pairs, i % pairs
        band, slot = pair // per_group, pair % per_group
        return band, order_ref[band * columns + group * per_group + slot]

    return pl.pallas_call(
        copy_block,
        grid_spec=pltpu.PrefetchScalarGridSpec(
            num_scalar_prefetch=1,
            grid=(groups * pairs,),
            in_specs=[pl.BlockSpec((1, sub_rows, block_size), lambda i, order_ref: (i, 0, 0))],
            out_specs=pl.BlockSpec((sub_rows, block_size), target),
        ),
        out_shape=jax.ShapeDtypeStruct((band_count * sub_rows, columns * block_size), pieces.dtype),
        name="natural_order",
    )(col_order.reshape(-1), pieces)


def local(grads, moments, factors, roots, refresh, owner):
    block_size = factors.shape[2]
    height = grads.shape[1]
    width_all = grads.shape[2]
    band_span = block_size // height
    groups = lax.axis_size("rep")
    columns = width_all // block_size
    per_group = columns // groups
    fsdp_count = lax.axis_size("fsdp")
    sub_rows = block_size // fsdp_count
    band_count = height // sub_rows
    half_cols = block_size // 2
    group_index = lax.axis_index("rep")
    fsdp_index = lax.axis_index("fsdp")
    band_index = fsdp_index // band_span
    local_index = fsdp_index % band_span
    side_index = local_index % 2
    slot_index = local_index // 2
    col_range = jnp.arange(columns, dtype=jnp.int32)
    col_order = jnp.argsort(owner * columns + col_range[None, :], axis=1)
    ordered = owner_order(grads[0], col_order, groups, band_count, sub_rows, block_size)
    summed = lax.psum_scatter(ordered, "rep", scatter_dimension=0, tiled=True)
    owned_grad = summed.reshape(band_count, per_group, sub_rows, block_size).astype(jnp.float32)
    gradient = jnp.transpose(owned_grad, (0, 2, 1, 3)) / groups
    moment_old = moments.reshape(band_count, sub_rows, per_group, block_size)
    moment_new = BETA_MOMENT * moment_old + (1.0 - BETA_MOMENT) * gradient * gradient
    adam_dir = gradient / (jnp.sqrt(moment_new) + EPS_ADAM)
    adam_table = jnp.sum(adam_dir * adam_dir, axis=(1, 3))
    pieces = (owned_grad / groups).astype(jnp.bfloat16).reshape(
        band_count * per_group, sub_rows, block_size
    )
    outgoing = jnp.repeat(pieces, 2, axis=0)
    incoming = lax.all_to_all(outgoing, "fsdp", split_axis=0, concat_axis=0, tiled=True)
    whole_block = incoming.reshape(block_size, block_size)
    operand = jnp.where(side_index == 0, whole_block, whole_block.T)
    gram_matrix = lax.dot_general(
        operand, operand, (((1,), (1,)), ((), ())), preferred_element_type=jnp.float32
    )
    new_factor = BETA_FACTOR * factors[0, 0] + (1.0 - BETA_FACTOR) * gram_matrix
    own_root = roots[0, 0]
    partner_root = from_partner(own_root, "fsdp", 0)
    left_root = jnp.where(side_index == 0, own_root, partner_root)
    right_root = jnp.where(side_index == 0, partner_root, own_root)
    right_cols = lax.dynamic_slice_in_dim(right_root, side_index * half_cols, half_cols, 1)
    mixed_rows = jnp.dot(left_root, whole_block, preferred_element_type=jnp.float32).astype(
        jnp.bfloat16
    )
    product = jnp.dot(mixed_rows, right_cols, preferred_element_type=jnp.float32)
    product_part = jnp.sum(product * product)
    band_mask = (jnp.arange(band_count) == band_index).astype(jnp.float32)[:, None]
    slot_mask = (jnp.arange(per_group) == slot_index).astype(jnp.float32)[None, :]
    product_table = band_mask * slot_mask * product_part
    adam_total, product_total = lax.psum((adam_table, product_table), "fsdp")
    adam_sq = jnp.sum(adam_total * band_mask * slot_mask)
    product_sq = jnp.sum(product_total * band_mask * slot_mask)
    graft_scale = jnp.sqrt(adam_sq) * lax.rsqrt(product_sq + EPS_NORM)
    update_half = (product * graft_scale).astype(jnp.bfloat16)
    outgoing_rows = update_half.reshape(fsdp_count, sub_rows, half_cols)
    incoming_rows = lax.all_to_all(outgoing_rows, "fsdp", split_axis=0, concat_axis=0, tiled=True)
    arranged_rows = incoming_rows.reshape(band_count, per_group, 2, sub_rows, half_cols)
    update_slab = jnp.transpose(arranged_rows, (0, 1, 3, 2, 4)).reshape(
        band_count * per_group, sub_rows, block_size
    )
    everything = lax.all_gather(update_slab, "rep", axis=0, tiled=True)
    update = natural_order(everything, col_order, groups, band_count, sub_rows, block_size)
    pair_ids = refresh // 2
    listed_band = pair_ids // columns
    listed_col = pair_ids % columns
    listed_rows = jnp.take(owner, listed_band, axis=0)
    listed_group = jnp.take_along_axis(listed_rows, listed_col[:, None], axis=1)[:, 0]
    listed_rank = jnp.sum(
        (
            (listed_rows == listed_group[:, None]) & (col_range[None, :] < listed_col[:, None])
        ).astype(jnp.int32),
        axis=1,
    )
    listed_fsdp = listed_band * band_span + 2 * listed_rank + refresh % 2
    chosen = jnp.any((listed_group == group_index) & (listed_fsdp == fsdp_index))
    new_root = lax.cond(chosen, newton_whole, lambda matrix: own_root, new_factor)
    new_moments = moment_new.reshape(height, per_group * block_size)
    return (update, new_moments, new_factor[None, None], new_root[None, None])


def solution(mesh):
    placed = (
        P("rep", "fsdp", None),
        P("fsdp", "rep"),
        P("rep", "fsdp", None, None),
        P("rep", "fsdp", None, None),
        P(),
        P(),
    )
    return jax.shard_map(
        local,
        mesh=mesh,
        in_specs=placed,
        out_specs=(
            P("fsdp", None),
            P("fsdp", "rep"),
            P("rep", "fsdp", None, None),
            P("rep", "fsdp", None, None),
        ),
        check_vma=False,
    )
```

```python
import functools

import jax
import jax.numpy as jnp
from jax import lax
from jax.experimental import pallas as pl
from jax.experimental.pallas import tpu as pltpu
from jax.sharding import PartitionSpec as P

NEWTON = 3


BETA_FACTOR = 0.9
BETA_MOMENT = 0.95
EPS_ADAM = 1e-08
EPS_NORM = 1e-06


def newton_seed(factor):
    norm_value = jnp.sqrt(jnp.sum(factor * factor))
    state_now = (factor / norm_value).astype(jnp.bfloat16)
    first_scale = norm_value ** (-0.25)
    return (state_now, first_scale)


def newton_step_matrix(state_now, identity):
    return ((5.0 * identity - state_now.astype(jnp.float32)) * 0.25).astype(jnp.bfloat16)


def newton_whole(factor):
    identity = jnp.eye(factor.shape[0], dtype=jnp.float32)
    state_now, first_scale = newton_seed(factor)
    root_now = (first_scale * identity).astype(jnp.bfloat16)
    for iteration in range(NEWTON):
        step_mat = newton_step_matrix(state_now, identity)
        root_now = jnp.dot(root_now, step_mat, preferred_element_type=jnp.float32).astype(
            jnp.bfloat16
        )
        if iteration + 1 < NEWTON:
            square = jnp.dot(step_mat, step_mat, preferred_element_type=jnp.float32).astype(
                jnp.bfloat16
            )
            fourth = jnp.dot(square, square, preferred_element_type=jnp.float32).astype(
                jnp.bfloat16
            )
            state_now = jnp.dot(fourth, state_now, preferred_element_type=jnp.float32).astype(
                jnp.bfloat16
            )
    return root_now


def move_blocks(steps, source, target, order_ref, in_ref, out_ref, held, in_sem, out_sem):
    def arrive(i):
        return pltpu.make_async_copy(source(i, order_ref, in_ref), held.at[i], in_sem.at[i])

    def leave(i):
        return pltpu.make_async_copy(held.at[i], target(i, order_ref, out_ref), out_sem.at[i])

    def pass_on(i):
        arrive(i).wait()
        leave(i).start()

    pl.loop(0, steps)(lambda i: arrive(i).start())
    pl.loop(0, steps)(pass_on)
    pl.loop(0, steps)(lambda i: leave(i).wait())


def move_call(steps, source, target, order, array, held_shape, out_shape, name):
    return pl.pallas_call(
        functools.partial(move_blocks, steps, source, target),
        in_specs=[pl.BlockSpec(memory_space=pltpu.SMEM), pl.BlockSpec(memory_space=pl.ANY)],
        out_specs=pl.BlockSpec(memory_space=pl.ANY),
        out_shape=jax.ShapeDtypeStruct(out_shape, array.dtype),
        scratch_shapes=[
            pltpu.VMEM((steps,) + held_shape, array.dtype),
            pltpu.SemaphoreType.DMA((steps,)),
            pltpu.SemaphoreType.DMA((steps,)),
        ],
        compiler_params=pltpu.CompilerParams(vmem_limit_bytes=16 << 20),
        name=name,
    )(order, array)


def owner_order(rows, order, groups, per_group, pairs, sub_rows, block_size):
    def source(i, order_ref, in_ref):
        pair, group = i // groups, i % groups
        band, slot = pair // per_group, pair % per_group
        col = order_ref[band * groups * per_group + group * per_group + slot]
        return in_ref.at[
            pl.ds(pl.multiple_of(band * sub_rows, sub_rows), sub_rows),
            pl.ds(pl.multiple_of(col * block_size, block_size), block_size),
        ]

    def target(i, order_ref, out_ref):
        return out_ref.at[i // groups, i % groups]

    shape = (sub_rows, block_size)
    return move_call(
        pairs * groups, source, target, order, rows, shape, (pairs, groups) + shape, "owner_order"
    )


def natural_order(pieces, order, groups, per_group, pairs, sub_rows, block_size):
    half = block_size // 2

    def source(i, order_ref, in_ref):
        return in_ref.at[i // (2 * pairs), (i // 2) % pairs, i % 2]

    def target(i, order_ref, out_ref):
        group, pair, side = i // (2 * pairs), (i // 2) % pairs, i % 2
        band, slot = pair // per_group, pair % per_group
        col = order_ref[band * groups * per_group + group * per_group + slot]
        return out_ref.at[
            pl.ds(pl.multiple_of(band * sub_rows, sub_rows), sub_rows),
            pl.ds(pl.multiple_of(col * block_size + side * half, half), half),
        ]

    out_shape = (pairs // per_group * sub_rows, groups * per_group * block_size)
    return move_call(
        groups * pairs * 2, source, target, order, pieces, (sub_rows, half), out_shape, "natural_order"
    )


def exchange_kernel(
    groups, count, per_group, grads_hbm, moments_hbm, root_hbm,
    upd, moments_out, block_out,
    gp, right_buf, left_buf, pieces, block, moments, roots, product, upd_half, adam_out, adam_in,
    square_sums,
    gp_sem, mom_sem, mom_out_sem, root_sem, block_sem, own_sem,
    right_send, right_recv, left_send, left_recv,
    piece_send, piece_recv, adam_send, adam_recv, root_send, root_recv, sq_send, sq_recv,
    upd_send, upd_recv, ag_right, ag_left, ag_recv,
):
    z, me = lax.axis_index("rep"), lax.axis_index("fsdp")
    pairs, _, sub_rows, size = gp.shape
    half = size // 2
    side, my_pair = me % 2, me // 2
    partner = me + 1 - 2 * side
    last = groups - 1

    def remote(src, dst, send, recv, **where):
        return pltpu.make_async_remote_copy(
            src_ref=src, dst_ref=dst, send_sem=send, recv_sem=recv,
            device_id=where, device_id_type=pl.DeviceIdType.MESH,
        )

    def load(k):
        return pltpu.make_async_copy(grads_hbm.at[k], gp.at[k], gp_sem.at[k])

    load(0).start()
    root_load = pltpu.make_async_copy(root_hbm, roots.at[side], root_sem)
    root_load.start()
    moments_load = pltpu.make_async_copy(moments_hbm, moments, mom_sem)
    moments_load.start()
    pl.loop(1, pairs)(lambda k: load(k).start())

    barrier = pltpu.get_barrier_semaphore()

    @pl.loop(1, count)
    def _(offset):
        pl.semaphore_signal(
            barrier, inc=1, device_id={"fsdp": (me + offset) % count},
            device_id_type=pl.DeviceIdType.MESH,
        )

    @pl.when(z > 0)
    def _():
        pl.semaphore_signal(
            barrier, inc=1, device_id={"rep": z - 1}, device_id_type=pl.DeviceIdType.MESH
        )

    @pl.when(z < last)
    def _():
        pl.semaphore_signal(
            barrier, inc=1, device_id={"rep": z + 1}, device_id_type=pl.DeviceIdType.MESH
        )

    pl.semaphore_wait(barrier, count - 1 + jnp.minimum(z, 1) + jnp.minimum(last - z, 1))

    def go_right(src, d, k):
        return remote(
            src, right_buf.at[k, d], right_send.at[k, d], right_recv.at[k, d],
            rep=jnp.minimum(z + 1, last),
        )

    def go_left(src, d, k):
        return remote(
            src, left_buf.at[k, d], left_send.at[k, d], left_recv.at[k, d],
            rep=jnp.maximum(z - 1, 0),
        )

    def send_raw(k):
        load(k).wait()
        for j in range(last):

            @pl.when(z == 0)
            def _():
                go_right(gp.at[k, last - j], last - j, k).start()

            @pl.when(z == last)
            def _():
                go_left(gp.at[k, j], j, k).start()

    def add_into(buf, k, d):
        buf[k, d] = (buf[k, d].astype(jnp.float32) + gp[k, d].astype(jnp.float32)).astype(buf.dtype)

    root_copy = remote(roots.at[side], roots.at[side], root_send, root_recv, fsdp=partner)

    def piece_copy(k, t):
        return remote(
            pieces.at[k], block.at[pl.ds(pl.multiple_of(me * sub_rows, sub_rows), sub_rows)],
            piece_send.at[k, t], piece_recv.at[me], fsdp=2 * k + t,
        )

    def adam_copy(k, t):
        return remote(
            adam_out.at[k], adam_in.at[me], adam_send.at[k, t], adam_recv.at[me], fsdp=2 * k + t
        )

    def reduce_slot(k):
        for j in range(last):
            far, near = last - j, j

            @pl.when((z > 0) & (z < far))
            def _():
                go_right(right_buf.at[k, far], far, k).wait_recv()
                add_into(right_buf, k, far)
                go_right(right_buf.at[k, far], far, k).start()

            @pl.when((z < last) & (z > near))
            def _():
                go_left(left_buf.at[k, near], near, k).wait_recv()
                add_into(left_buf, k, near)
                go_left(left_buf.at[k, near], near, k).start()

        @pl.when(z > 0)
        def _():
            go_right(right_buf.at[k, z], z, k).wait_recv()

        @pl.when(z < last)
        def _():
            go_left(left_buf.at[k, z], z, k).wait_recv()

        @pl.when(k == 0)
        def _():
            moments_load.wait()

        band, slot = k // per_group, k % per_group
        cols = pl.ds(pl.multiple_of(slot * size, size), size)

        def rows_step(i, total):
            part = pl.ds(pl.multiple_of(i * 16, 16), 16)
            rows = pl.ds(pl.multiple_of(band * sub_rows + i * 16, 16), 16)
            own = gp[k, z, part, :].astype(jnp.float32)
            from_left = right_buf[k, z, part, :].astype(jnp.float32)
            from_right = left_buf[k, z, part, :].astype(jnp.float32)
            own = own + jnp.where(z > 0, from_left, 0.0) + jnp.where(z < last, from_right, 0.0)
            gradient = own / groups
            moment = BETA_MOMENT * moments[rows, cols] + (1.0 - BETA_MOMENT) * gradient * gradient
            moments[rows, cols] = moment
            pieces[k, part, :] = gradient.astype(jnp.bfloat16)
            step = gradient / (jnp.sqrt(moment) + EPS_ADAM)
            return total + step * step

        total = lax.fori_loop(
            0, sub_rows // 16, rows_step, jnp.zeros((16, size), jnp.float32), unroll=2
        )
        adam_out[k] = jnp.full((8, 128), jnp.sum(total), jnp.float32)
        for t in range(2):

            @pl.when(me != 2 * k + t)
            def _():
                piece_copy(k, t).start()
                adam_copy(k, t).start()

        @pl.when(my_pair == k)
        def _():
            block[pl.ds(pl.multiple_of(me * sub_rows, sub_rows), sub_rows), :] = pieces[k]
            adam_in[me] = adam_out[k]

    tile = 256

    def own_slot(k):
        @pl.loop(0, count)
        def _(f):
            @pl.when(f != me)
            def _():
                remote(
                    pieces.at[k], block.at[pl.ds(pl.multiple_of(f * sub_rows, sub_rows), sub_rows)],
                    piece_send.at[k, 0], piece_recv.at[f], fsdp=partner,
                ).wait_recv()
                remote(
                    adam_out.at[k], adam_in.at[f], adam_send.at[k, 0], adam_recv.at[f], fsdp=partner
                ).wait_recv()

        root_copy_in = remote(
            roots.at[1 - side], roots.at[1 - side], root_send, root_recv, fsdp=partner
        )
        root_copy_in.wait_recv()
        pltpu.make_async_copy(block, block_out, block_sem).start()
        half_cols = pl.ds(pl.multiple_of(side * half, half), half)

        def multiply(i, total):
            rows = pl.ds(pl.multiple_of(i * tile, tile), tile)
            mixed = jnp.dot(
                roots[0, rows, :], block[...], preferred_element_type=jnp.float32
            ).astype(jnp.bfloat16)
            result = jnp.dot(mixed, roots[1, :, half_cols], preferred_element_type=jnp.float32)
            product[rows, :] = result
            return total + jnp.sum(result * result)

        total = lax.fori_loop(0, size // tile, multiply, jnp.float32(0.0))
        square_sums[side] = jnp.full((8, 128), total, jnp.float32)
        remote(square_sums.at[side], square_sums.at[side], sq_send, sq_recv, fsdp=partner).start()
        remote(
            square_sums.at[1 - side], square_sums.at[1 - side], sq_send, sq_recv, fsdp=partner
        ).wait_recv()
        product_sq = square_sums[0] + square_sums[1]
        adam_sq = jnp.sum(adam_in[...], axis=0)
        scale = (jnp.sqrt(adam_sq) * lax.rsqrt(product_sq + EPS_NORM))[:1, :1]

        @pl.loop(0, count)
        def _(step):
            f = (me + step) % count
            rows = pl.ds(pl.multiple_of(f * sub_rows, sub_rows), sub_rows)
            upd_half[rows, :] = (product[rows, :] * scale).astype(jnp.bfloat16)

            @pl.when(f != me)
            def _():
                remote(
                    upd_half.at[rows], upd.at[z, k, side], upd_send.at[f], upd_recv.at[k, side],
                    fsdp=f,
                ).start()

            @pl.when(f == me)
            def _():
                pltpu.make_async_copy(upd_half.at[rows], upd.at[z, k, side], own_sem).start()

    def pass_right(s, k):
        return remote(
            upd.at[s, k], upd.at[s, k], ag_right.at[s, k], ag_recv.at[s, k],
            rep=jnp.minimum(z + 1, last),
        )

    def pass_left(s, k):
        return remote(
            upd.at[s, k], upd.at[s, k], ag_left.at[s, k], ag_recv.at[s, k],
            rep=jnp.maximum(z - 1, 0),
        )

    def gather_slot(k):
        for t in range(2):

            @pl.when(me == 2 * k + t)
            def _():
                pltpu.make_async_copy(
                    upd_half.at[pl.ds(pl.multiple_of(me * sub_rows, sub_rows), sub_rows)],
                    upd.at[z, k, t], own_sem,
                ).wait()

            @pl.when(me != 2 * k + t)
            def _():
                remote(
                    upd_half.at[pl.ds(0, sub_rows)], upd.at[z, k, t], upd_send.at[0],
                    upd_recv.at[k, t], fsdp=partner,
                ).wait_recv()

        @pl.when(z < last)
        def _():
            pass_right(z, k).start()

        @pl.when(z > 0)
        def _():
            pass_left(z, k).start()

        for j in range(1, groups):

            @pl.when(z - j >= 0)
            def _():
                s = z - j
                pass_right(s, k).wait_recv()

                @pl.when(z < last)
                def _():
                    pass_right(s, k).start()

            @pl.when(z + j <= last)
            def _():
                s = z + j
                pass_left(s, k).wait_recv()

                @pl.when(z > 0)
                def _():
                    pass_left(s, k).start()

    send_raw(0)
    root_load.wait()
    root_copy.start()

    @pl.loop(0, pairs + 2)
    def _(t):
        @pl.when(t + 1 < pairs)
        def _():
            send_raw(t + 1)

        @pl.when(t < pairs)
        def _():
            reduce_slot(t)

        @pl.when(my_pair == t - 1)
        def _():
            own_slot(t - 1)

        @pl.when(t == pairs)
        def _():
            pltpu.make_async_copy(moments, moments_out, mom_out_sem).start()

        @pl.when(t >= 2)
        def _():
            gather_slot(t - 2)

    root_copy.wait_send()
    remote(square_sums.at[side], square_sums.at[side], sq_send, sq_recv, fsdp=partner).wait_send()
    pltpu.make_async_copy(moments, moments_out, mom_out_sem).wait()
    pltpu.make_async_copy(block, block_out, block_sem).wait()

    @pl.loop(0, count)
    def _(f):
        @pl.when(f != me)
        def _():
            rows = pl.ds(pl.multiple_of(f * sub_rows, sub_rows), sub_rows)
            remote(
                upd_half.at[rows], upd.at[z, my_pair, side], upd_send.at[f],
                upd_recv.at[my_pair, side], fsdp=f,
            ).wait_send()

    @pl.loop(0, pairs)
    def _(k):
        for t in range(2):

            @pl.when(me != 2 * k + t)
            def _():
                piece_copy(k, t).wait_send()
                adam_copy(k, t).wait_send()

        for d in range(groups):

            @pl.when(z < d)
            def _():
                go_right(right_buf.at[k, d], d, k).wait_send()

            @pl.when(z > d)
            def _():
                go_left(left_buf.at[k, d], d, k).wait_send()

            @pl.when((d <= z) & (z < last))
            def _():
                pass_right(d, k).wait_send()

            @pl.when((d >= z) & (z > 0))
            def _():
                pass_left(d, k).wait_send()


def exchange(ordered, moments, root, per_group, count):
    pairs, groups, sub_rows, size = ordered.shape
    half = size // 2
    low, wide = jnp.bfloat16, jnp.float32
    dma = pltpu.SemaphoreType.DMA
    anywhere = pl.BlockSpec(memory_space=pl.ANY)
    return pl.pallas_call(
        functools.partial(exchange_kernel, groups, count, per_group),
        in_specs=[anywhere] * 3,
        out_specs=[anywhere] * 3,
        out_shape=[
            jax.ShapeDtypeStruct((groups, pairs, 2, sub_rows, half), low),
            jax.ShapeDtypeStruct(moments.shape, wide),
            jax.ShapeDtypeStruct((size, size), low),
        ],
        scratch_shapes=[
            pltpu.VMEM((pairs, groups, sub_rows, size), low),
            pltpu.VMEM((pairs, groups, sub_rows, size), low),
            pltpu.VMEM((pairs, groups, sub_rows, size), low),
            pltpu.VMEM((pairs, sub_rows, size), low),
            pltpu.VMEM((size, size), low),
            pltpu.VMEM(moments.shape, wide),
            pltpu.VMEM((2, size, size), low),
            pltpu.VMEM((size, half), wide),
            pltpu.VMEM((size, half), low),
            pltpu.VMEM((pairs, 8, 128), wide),
            pltpu.VMEM((count, 8, 128), wide),
            pltpu.VMEM((2, 8, 128), wide),
            dma((pairs,)), dma, dma, dma, dma, dma,
            dma((pairs, groups)), dma((pairs, groups)), dma((pairs, groups)), dma((pairs, groups)),
            dma((pairs, 2)), dma((count,)), dma((pairs, 2)), dma((count,)), dma, dma, dma, dma,
            dma((count,)), dma((pairs, 2)), dma((groups, pairs)), dma((groups, pairs)),
            dma((groups, pairs)),
        ],
        compiler_params=pltpu.CompilerParams(
            collective_id=0, has_side_effects=True, vmem_limit_bytes=48 << 20
        ),
        name="exchange",
    )(ordered, moments, root)


def local(grads, moments, factors, roots, refresh, owner):
    block_size = factors.shape[2]
    height = grads.shape[1]
    width_all = grads.shape[2]
    band_span = block_size // height
    groups = lax.axis_size("rep")
    columns = width_all // block_size
    per_group = columns // groups
    fsdp_count = lax.axis_size("fsdp")
    sub_rows = block_size // fsdp_count
    band_count = height // sub_rows
    half_cols = block_size // 2
    group_index = lax.axis_index("rep")
    fsdp_index = lax.axis_index("fsdp")
    band_index = fsdp_index // band_span
    local_index = fsdp_index % band_span
    side_index = local_index % 2
    slot_index = local_index // 2
    col_range = jnp.arange(columns, dtype=jnp.int32)
    col_order = jnp.argsort(owner * columns + col_range[None, :], axis=1)
    pairs = band_count * per_group
    order = col_order.reshape(-1).astype(jnp.int32)
    ordered = owner_order(grads[0], order, groups, per_group, pairs, sub_rows, block_size)
    own_root = roots[0, 0]
    gathered, new_moments, whole_block = exchange(ordered, moments, own_root, per_group, fsdp_count)
    update = natural_order(gathered, order, groups, per_group, pairs, sub_rows, block_size)
    operand = jnp.where(side_index == 0, whole_block, whole_block.T)
    gram_matrix = lax.dot_general(
        operand, operand, (((1,), (1,)), ((), ())), preferred_element_type=jnp.float32
    )
    new_factor = BETA_FACTOR * factors[0, 0] + (1.0 - BETA_FACTOR) * gram_matrix
    pair_ids = refresh // 2
    listed_band = pair_ids // columns
    listed_col = pair_ids % columns
    listed_rows = jnp.take(owner, listed_band, axis=0)
    listed_group = jnp.take_along_axis(listed_rows, listed_col[:, None], axis=1)[:, 0]
    listed_rank = jnp.sum(
        (
            (listed_rows == listed_group[:, None]) & (col_range[None, :] < listed_col[:, None])
        ).astype(jnp.int32),
        axis=1,
    )
    listed_fsdp = listed_band * band_span + 2 * listed_rank + refresh % 2
    chosen = jnp.any((listed_group == group_index) & (listed_fsdp == fsdp_index))
    new_root = lax.cond(chosen, newton_whole, lambda matrix: own_root, new_factor)
    return (update, new_moments, new_factor[None, None], new_root[None, None])


def solution(mesh):
    placed = (
        P("rep", "fsdp", None),
        P("fsdp", "rep"),
        P("rep", "fsdp", None, None),
        P("rep", "fsdp", None, None),
        P(),
        P(),
    )
    return jax.shard_map(
        local,
        mesh=mesh,
        in_specs=placed,
        out_specs=(
            P("fsdp", None),
            P("fsdp", "rep"),
            P("rep", "fsdp", None, None),
            P("rep", "fsdp", None, None),
        ),
        check_vma=False,
    )
```

```python
import functools

import jax
import jax.numpy as jnp
from jax import lax
from jax.experimental import pallas as pl
from jax.experimental.pallas import tpu as pltpu
from jax.sharding import PartitionSpec as P

NEWTON = 3


BETA_FACTOR = 0.9
BETA_MOMENT = 0.95
EPS_ADAM = 1e-08
EPS_NORM = 1e-06


def move_blocks(steps, source, target, order_ref, in_ref, out_ref, held, in_sem, out_sem):
    def arrive(i):
        return pltpu.make_async_copy(source(i, order_ref, in_ref), held.at[i], in_sem.at[i])

    def leave(i):
        return pltpu.make_async_copy(held.at[i], target(i, order_ref, out_ref), out_sem.at[i])

    def pass_on(i):
        arrive(i).wait()
        leave(i).start()

    pl.loop(0, steps)(lambda i: arrive(i).start())
    pl.loop(0, steps)(pass_on)
    pl.loop(0, steps)(lambda i: leave(i).wait())


def move_call(steps, source, target, order, array, held_shape, out_shape, name):
    return pl.pallas_call(
        functools.partial(move_blocks, steps, source, target),
        in_specs=[pl.BlockSpec(memory_space=pltpu.SMEM), pl.BlockSpec(memory_space=pl.ANY)],
        out_specs=pl.BlockSpec(memory_space=pl.ANY),
        out_shape=jax.ShapeDtypeStruct(out_shape, array.dtype),
        scratch_shapes=[
            pltpu.VMEM((steps,) + held_shape, array.dtype),
            pltpu.SemaphoreType.DMA((steps,)),
            pltpu.SemaphoreType.DMA((steps,)),
        ],
        compiler_params=pltpu.CompilerParams(vmem_limit_bytes=16 << 20),
        name=name,
    )(order, array)


def owner_order(rows, order, groups, per_group, pairs, sub_rows, block_size):
    def source(i, order_ref, in_ref):
        pair, group = i // groups, i % groups
        band, slot = pair // per_group, pair % per_group
        col = order_ref[band * groups * per_group + group * per_group + slot]
        return in_ref.at[
            pl.ds(pl.multiple_of(band * sub_rows, sub_rows), sub_rows),
            pl.ds(pl.multiple_of(col * block_size, block_size), block_size),
        ]

    def target(i, order_ref, out_ref):
        return out_ref.at[i // groups, i % groups]

    shape = (sub_rows, block_size)
    return move_call(
        pairs * groups, source, target, order, rows, shape, (pairs, groups) + shape, "owner_order"
    )


def natural_order(pieces, order, groups, per_group, pairs, sub_rows, block_size):
    half = block_size // 2

    def source(i, order_ref, in_ref):
        return in_ref.at[i // (2 * pairs), (i // 2) % pairs, i % 2]

    def target(i, order_ref, out_ref):
        group, pair, side = i // (2 * pairs), (i // 2) % pairs, i % 2
        band, slot = pair // per_group, pair % per_group
        col = order_ref[band * groups * per_group + group * per_group + slot]
        return out_ref.at[
            pl.ds(pl.multiple_of(band * sub_rows, sub_rows), sub_rows),
            pl.ds(pl.multiple_of(col * block_size + side * half, half), half),
        ]

    out_shape = (pairs // per_group * sub_rows, groups * per_group * block_size)
    return move_call(
        groups * pairs * 2, source, target, order, pieces, (sub_rows, half), out_shape, "natural_order"
    )


def exchange_kernel(
    groups, count, per_group, grads_hbm, moments_hbm, root_hbm, factor_hbm,
    upd, moments_out, factor_out, root_out,
    gp, right_buf, left_buf, pieces, block, moments, roots, product, upd_half, adam_out, adam_in,
    square_sums, factor, newton, norm,
    gp_sem, mom_sem, mom_out_sem, root_sem, factor_sem, factor_out_sem, root_out_sem, own_sem,
    right_send, right_recv, left_send, left_recv,
    piece_send, piece_recv, adam_send, adam_recv, root_send, root_recv, sq_send, sq_recv,
    upd_send, upd_recv, ag_right, ag_left, ag_recv,
):
    z, me = lax.axis_index("rep"), lax.axis_index("fsdp")
    pairs, _, sub_rows, size = gp.shape
    half = size // 2
    side, my_pair = me % 2, me // 2
    partner = me + 1 - 2 * side
    last = groups - 1

    def remote(src, dst, send, recv, **where):
        return pltpu.make_async_remote_copy(
            src_ref=src, dst_ref=dst, send_sem=send, recv_sem=recv,
            device_id=where, device_id_type=pl.DeviceIdType.MESH,
        )

    def load(k):
        return pltpu.make_async_copy(grads_hbm.at[k], gp.at[k], gp_sem.at[k])

    load(0).start()
    root_load = pltpu.make_async_copy(root_hbm, roots.at[side], root_sem)
    root_load.start()
    moments_load = pltpu.make_async_copy(moments_hbm, moments, mom_sem)
    moments_load.start()
    factor_load = pltpu.make_async_copy(factor_hbm, factor, factor_sem)
    factor_load.start()
    pl.loop(1, pairs)(lambda k: load(k).start())

    barrier = pltpu.get_barrier_semaphore()

    @pl.loop(1, count)
    def _(offset):
        pl.semaphore_signal(
            barrier, inc=1, device_id={"fsdp": (me + offset) % count},
            device_id_type=pl.DeviceIdType.MESH,
        )

    @pl.when(z > 0)
    def _():
        pl.semaphore_signal(
            barrier, inc=1, device_id={"rep": z - 1}, device_id_type=pl.DeviceIdType.MESH
        )

    @pl.when(z < last)
    def _():
        pl.semaphore_signal(
            barrier, inc=1, device_id={"rep": z + 1}, device_id_type=pl.DeviceIdType.MESH
        )

    pl.semaphore_wait(barrier, count - 1 + jnp.minimum(z, 1) + jnp.minimum(last - z, 1))

    def go_right(src, d, k):
        return remote(
            src, right_buf.at[k, d], right_send.at[k, d], right_recv.at[k, d],
            rep=jnp.minimum(z + 1, last),
        )

    def go_left(src, d, k):
        return remote(
            src, left_buf.at[k, d], left_send.at[k, d], left_recv.at[k, d],
            rep=jnp.maximum(z - 1, 0),
        )

    def send_raw(k):
        load(k).wait()
        for j in range(last):

            @pl.when(z == 0)
            def _():
                go_right(gp.at[k, last - j], last - j, k).start()

            @pl.when(z == last)
            def _():
                go_left(gp.at[k, j], j, k).start()

    def add_into(buf, k, d):
        buf[k, d] = (buf[k, d].astype(jnp.float32) + gp[k, d].astype(jnp.float32)).astype(buf.dtype)

    root_copy = remote(roots.at[side], roots.at[side], root_send, root_recv, fsdp=partner)

    def piece_copy(k, t):
        return remote(
            pieces.at[k], block.at[pl.ds(pl.multiple_of(me * sub_rows, sub_rows), sub_rows)],
            piece_send.at[k, t], piece_recv.at[me], fsdp=2 * k + t,
        )

    def adam_copy(k, t):
        return remote(
            adam_out.at[k], adam_in.at[me], adam_send.at[k, t], adam_recv.at[me], fsdp=2 * k + t
        )

    def reduce_slot(k):
        for j in range(last):
            far, near = last - j, j

            @pl.when((z > 0) & (z < far))
            def _():
                go_right(right_buf.at[k, far], far, k).wait_recv()
                add_into(right_buf, k, far)
                go_right(right_buf.at[k, far], far, k).start()

            @pl.when((z < last) & (z > near))
            def _():
                go_left(left_buf.at[k, near], near, k).wait_recv()
                add_into(left_buf, k, near)
                go_left(left_buf.at[k, near], near, k).start()

        @pl.when(z > 0)
        def _():
            go_right(right_buf.at[k, z], z, k).wait_recv()

        @pl.when(z < last)
        def _():
            go_left(left_buf.at[k, z], z, k).wait_recv()

        @pl.when(k == 0)
        def _():
            moments_load.wait()

        band, slot = k // per_group, k % per_group
        cols = pl.ds(pl.multiple_of(slot * size, size), size)

        def rows_step(i, total):
            part = pl.ds(pl.multiple_of(i * 16, 16), 16)
            rows = pl.ds(pl.multiple_of(band * sub_rows + i * 16, 16), 16)
            own = gp[k, z, part, :].astype(jnp.float32)
            from_left = right_buf[k, z, part, :].astype(jnp.float32)
            from_right = left_buf[k, z, part, :].astype(jnp.float32)
            own = own + jnp.where(z > 0, from_left, 0.0) + jnp.where(z < last, from_right, 0.0)
            gradient = own / groups
            moment = BETA_MOMENT * moments[rows, cols] + (1.0 - BETA_MOMENT) * gradient * gradient
            moments[rows, cols] = moment
            pieces[k, part, :] = gradient.astype(jnp.bfloat16)
            step = gradient / (jnp.sqrt(moment) + EPS_ADAM)
            return total + step * step

        total = lax.fori_loop(
            0, sub_rows // 16, rows_step, jnp.zeros((16, size), jnp.float32), unroll=2
        )
        adam_out[k] = jnp.full((8, 128), jnp.sum(total), jnp.float32)
        for t in range(2):

            @pl.when(me != 2 * k + t)
            def _():
                piece_copy(k, t).start()
                adam_copy(k, t).start()

        @pl.when(my_pair == k)
        def _():
            block[pl.ds(pl.multiple_of(me * sub_rows, sub_rows), sub_rows), :] = pieces[k]
            adam_in[me] = adam_out[k]

    tile = 256

    def own_slot(k):
        @pl.loop(0, count)
        def _(f):
            @pl.when(f != me)
            def _():
                remote(
                    pieces.at[k], block.at[pl.ds(pl.multiple_of(f * sub_rows, sub_rows), sub_rows)],
                    piece_send.at[k, 0], piece_recv.at[f], fsdp=partner,
                ).wait_recv()
                remote(
                    adam_out.at[k], adam_in.at[f], adam_send.at[k, 0], adam_recv.at[f], fsdp=partner
                ).wait_recv()

        root_copy_in = remote(
            roots.at[1 - side], roots.at[1 - side], root_send, root_recv, fsdp=partner
        )
        root_copy_in.wait_recv()
        half_cols = pl.ds(pl.multiple_of(side * half, half), half)

        def multiply(i, total):
            rows = pl.ds(pl.multiple_of(i * tile, tile), tile)
            mixed = jnp.dot(
                roots[0, rows, :], block[...], preferred_element_type=jnp.float32
            ).astype(jnp.bfloat16)
            result = jnp.dot(mixed, roots[1, :, half_cols], preferred_element_type=jnp.float32)
            product[rows, :] = result
            return total + jnp.sum(result * result)

        total = lax.fori_loop(0, size // tile, multiply, jnp.float32(0.0))
        square_sums[side] = jnp.full((8, 128), total, jnp.float32)
        remote(square_sums.at[side], square_sums.at[side], sq_send, sq_recv, fsdp=partner).start()
        remote(
            square_sums.at[1 - side], square_sums.at[1 - side], sq_send, sq_recv, fsdp=partner
        ).wait_recv()
        product_sq = square_sums[0] + square_sums[1]
        adam_sq = jnp.sum(adam_in[...], axis=0)
        scale = (jnp.sqrt(adam_sq) * lax.rsqrt(product_sq + EPS_NORM))[:1, :1]

        @pl.loop(0, count)
        def _(step):
            f = (me + step) % count
            rows = pl.ds(pl.multiple_of(f * sub_rows, sub_rows), sub_rows)
            upd_half[rows, :] = (product[rows, :] * scale).astype(jnp.bfloat16)

            @pl.when(f != me)
            def _():
                remote(
                    upd_half.at[rows], upd.at[z, k, side], upd_send.at[f], upd_recv.at[k, side],
                    fsdp=f,
                ).start()

            @pl.when(f == me)
            def _():
                pltpu.make_async_copy(upd_half.at[rows], upd.at[z, k, side], own_sem).start()

    def pass_right(s, k):
        return remote(
            upd.at[s, k], upd.at[s, k], ag_right.at[s, k], ag_recv.at[s, k],
            rep=jnp.minimum(z + 1, last),
        )

    def pass_left(s, k):
        return remote(
            upd.at[s, k], upd.at[s, k], ag_left.at[s, k], ag_recv.at[s, k],
            rep=jnp.maximum(z - 1, 0),
        )

    def tiles(body):
        pl.loop(0, size // tile)(lambda i: body(pl.ds(pl.multiple_of(i * tile, tile), tile)))

    def times(dst, lhs, rhs):
        @tiles
        def _(rows):
            newton[dst, rows, :] = jnp.dot(
                newton[lhs, rows, :], newton[rhs], preferred_element_type=jnp.float32
            ).astype(jnp.bfloat16)

    def step_rows(rows, state):
        shape = (tile, size)
        on_diagonal = lax.broadcasted_iota(jnp.int32, shape, 0) + rows.start == (
            lax.broadcasted_iota(jnp.int32, shape, 1)
        )
        return ((jnp.where(on_diagonal, 5.0, 0.0) - state.astype(jnp.float32)) * 0.25).astype(
            jnp.bfloat16
        )

    def step_from(state):
        @tiles
        def _(rows):
            newton[1, rows, :] = step_rows(rows, newton[state, rows, :])

    def gram():
        factor_load.wait()

        @pl.when(side == 0)
        def _():
            @tiles
            def _(rows):
                newton[3, rows, :] = block[rows, :]

        @pl.when(side == 1)
        def _():
            @tiles
            def _(rows):
                newton[3, :, rows] = block[rows, :].T

        def add_gram(i, total):
            rows = pl.ds(pl.multiple_of(i * tile, tile), tile)
            product_rows = lax.dot_general(
                newton[3, rows, :], newton[3], (((1,), (1,)), ((), ())),
                preferred_element_type=jnp.float32,
            )
            new = BETA_FACTOR * factor[rows, :] + (1.0 - BETA_FACTOR) * product_rows
            factor[rows, :] = new
            return total + jnp.sum(new * new)

        total = lax.fori_loop(0, size // tile, add_gram, jnp.float32(0.0))
        norm[...] = jnp.sqrt(jnp.full((8, 128), total, jnp.float32))
        pltpu.make_async_copy(factor, factor_out, factor_out_sem).start()

    def seed():
        z_norm = norm[...]
        first = lax.rsqrt(jnp.sqrt(z_norm))[:1, :1].astype(jnp.bfloat16).astype(jnp.float32)

        @tiles
        def _(rows):
            state = (factor[rows, :] / z_norm[:1, :1]).astype(jnp.bfloat16)
            newton[0, rows, :] = state
            step_mat = step_rows(rows, state)
            newton[1, rows, :] = step_mat
            newton[4, rows, :] = (first * step_mat.astype(jnp.float32)).astype(jnp.bfloat16)

    def first_state():
        times(2, 3, 0)
        step_from(2)

    def second_state():
        times(3, 4, 2)
        step_from(3)

    def finish():
        times(2, 0, 1)
        pltpu.make_async_copy(newton.at[2], root_out, root_out_sem).start()

    stages = [
        gram, seed, lambda: times(2, 1, 1), lambda: times(3, 2, 2), first_state,
        lambda: times(0, 4, 1), lambda: times(3, 1, 1), lambda: times(4, 3, 3), second_state,
        finish,
    ]

    def gather_slot(k, fill=lambda j: None):
        for t in range(2):

            @pl.when(me == 2 * k + t)
            def _():
                pltpu.make_async_copy(
                    upd_half.at[pl.ds(pl.multiple_of(me * sub_rows, sub_rows), sub_rows)],
                    upd.at[z, k, t], own_sem,
                ).wait()

            @pl.when(me != 2 * k + t)
            def _():
                remote(
                    upd_half.at[pl.ds(0, sub_rows)], upd.at[z, k, t], upd_send.at[0],
                    upd_recv.at[k, t], fsdp=partner,
                ).wait_recv()

        @pl.when(z < last)
        def _():
            pass_right(z, k).start()

        @pl.when(z > 0)
        def _():
            pass_left(z, k).start()

        for j in range(1, groups):
            fill(j)

            @pl.when(z - j >= 0)
            def _():
                s = z - j
                pass_right(s, k).wait_recv()

                @pl.when(z < last)
                def _():
                    pass_right(s, k).start()

            @pl.when(z + j <= last)
            def _():
                s = z + j
                pass_left(s, k).wait_recv()

                @pl.when(z > 0)
                def _():
                    pass_left(s, k).start()

    send_raw(0)
    root_load.wait()
    root_copy.start()
    send_raw(1)

    @pl.loop(0, pairs)
    def _(t):
        @pl.when(t + 2 < pairs)
        def _():
            send_raw(t + 2)

        reduce_slot(t)

        @pl.when(my_pair == t - 1)
        def _():
            own_slot(t - 1)

        @pl.when(t >= 2)
        def _():
            gather_slot(t - 2)

    pltpu.make_async_copy(moments, moments_out, mom_out_sem).start()

    @pl.when(my_pair == pairs - 1)
    def _():
        own_slot(pairs - 1)

    def fill_early(j):
        if j < 3:
            stages[j - 1]()

    def fill_late(j):
        for stage in stages[j + 1:j + 2] if j < groups - 1 else stages[j + 1:]:
            stage()

    gather_slot(pairs - 2, fill_early)
    gather_slot(pairs - 1, fill_late)
    root_copy.wait_send()
    remote(square_sums.at[side], square_sums.at[side], sq_send, sq_recv, fsdp=partner).wait_send()
    pltpu.make_async_copy(moments, moments_out, mom_out_sem).wait()
    pltpu.make_async_copy(factor, factor_out, factor_out_sem).wait()
    pltpu.make_async_copy(newton.at[2], root_out, root_out_sem).wait()

    @pl.loop(0, count)
    def _(f):
        @pl.when(f != me)
        def _():
            rows = pl.ds(pl.multiple_of(f * sub_rows, sub_rows), sub_rows)
            remote(
                upd_half.at[rows], upd.at[z, my_pair, side], upd_send.at[f],
                upd_recv.at[my_pair, side], fsdp=f,
            ).wait_send()

    @pl.loop(0, pairs)
    def _(k):
        for t in range(2):

            @pl.when(me != 2 * k + t)
            def _():
                piece_copy(k, t).wait_send()
                adam_copy(k, t).wait_send()

        for d in range(groups):

            @pl.when(z < d)
            def _():
                go_right(right_buf.at[k, d], d, k).wait_send()

            @pl.when(z > d)
            def _():
                go_left(left_buf.at[k, d], d, k).wait_send()

            @pl.when((d <= z) & (z < last))
            def _():
                pass_right(d, k).wait_send()

            @pl.when((d >= z) & (z > 0))
            def _():
                pass_left(d, k).wait_send()


def exchange(ordered, moments, root, factor, per_group, count):
    pairs, groups, sub_rows, size = ordered.shape
    half = size // 2
    low, wide = jnp.bfloat16, jnp.float32
    dma = pltpu.SemaphoreType.DMA
    anywhere = pl.BlockSpec(memory_space=pl.ANY)
    return pl.pallas_call(
        functools.partial(exchange_kernel, groups, count, per_group),
        in_specs=[anywhere] * 4,
        out_specs=[anywhere] * 4,
        out_shape=[
            jax.ShapeDtypeStruct((groups, pairs, 2, sub_rows, half), low),
            jax.ShapeDtypeStruct(moments.shape, wide),
            jax.ShapeDtypeStruct((size, size), wide),
            jax.ShapeDtypeStruct((size, size), low),
        ],
        scratch_shapes=[
            pltpu.VMEM((pairs, groups, sub_rows, size), low),
            pltpu.VMEM((pairs, groups, sub_rows, size), low),
            pltpu.VMEM((pairs, groups, sub_rows, size), low),
            pltpu.VMEM((pairs, sub_rows, size), low),
            pltpu.VMEM((size, size), low),
            pltpu.VMEM(moments.shape, wide),
            pltpu.VMEM((2, size, size), low),
            pltpu.VMEM((size, half), wide),
            pltpu.VMEM((size, half), low),
            pltpu.VMEM((pairs, 8, 128), wide),
            pltpu.VMEM((count, 8, 128), wide),
            pltpu.VMEM((2, 8, 128), wide),
            pltpu.VMEM((size, size), wide),
            pltpu.VMEM((5, size, size), low),
            pltpu.VMEM((8, 128), wide),
            dma((pairs,)), dma, dma, dma, dma, dma, dma, dma,
            dma((pairs, groups)), dma((pairs, groups)), dma((pairs, groups)), dma((pairs, groups)),
            dma((pairs, 2)), dma((count,)), dma((pairs, 2)), dma((count,)), dma, dma, dma, dma,
            dma((count,)), dma((pairs, 2)), dma((groups, pairs)), dma((groups, pairs)),
            dma((groups, pairs)),
        ],
        compiler_params=pltpu.CompilerParams(
            collective_id=0, has_side_effects=True, vmem_limit_bytes=56 << 20
        ),
        name="exchange",
    )(ordered, moments, root, factor)


def local(grads, moments, factors, roots, refresh, owner):
    block_size = factors.shape[2]
    height = grads.shape[1]
    width_all = grads.shape[2]
    band_span = block_size // height
    groups = lax.axis_size("rep")
    columns = width_all // block_size
    per_group = columns // groups
    fsdp_count = lax.axis_size("fsdp")
    sub_rows = block_size // fsdp_count
    band_count = height // sub_rows
    half_cols = block_size // 2
    group_index = lax.axis_index("rep")
    fsdp_index = lax.axis_index("fsdp")
    band_index = fsdp_index // band_span
    local_index = fsdp_index % band_span
    side_index = local_index % 2
    slot_index = local_index // 2
    col_range = jnp.arange(columns, dtype=jnp.int32)
    col_order = jnp.argsort(owner * columns + col_range[None, :], axis=1)
    pairs = band_count * per_group
    order = col_order.reshape(-1).astype(jnp.int32)
    ordered = owner_order(grads[0], order, groups, per_group, pairs, sub_rows, block_size)
    own_root = roots[0, 0]
    gathered, new_moments, new_factor, fresh_root = exchange(
        ordered, moments, own_root, factors[0, 0], per_group, fsdp_count
    )
    update = natural_order(gathered, order, groups, per_group, pairs, sub_rows, block_size)
    pair_ids = refresh // 2
    listed_band = pair_ids // columns
    listed_col = pair_ids % columns
    listed_rows = jnp.take(owner, listed_band, axis=0)
    listed_group = jnp.take_along_axis(listed_rows, listed_col[:, None], axis=1)[:, 0]
    listed_rank = jnp.sum(
        (
            (listed_rows == listed_group[:, None]) & (col_range[None, :] < listed_col[:, None])
        ).astype(jnp.int32),
        axis=1,
    )
    listed_fsdp = listed_band * band_span + 2 * listed_rank + refresh % 2
    chosen = jnp.any((listed_group == group_index) & (listed_fsdp == fsdp_index))
    new_root = jnp.where(chosen, fresh_root, own_root)
    return (update, new_moments, new_factor[None, None], new_root[None, None])


def solution(mesh):
    placed = (
        P("rep", "fsdp", None),
        P("fsdp", "rep"),
        P("rep", "fsdp", None, None),
        P("rep", "fsdp", None, None),
        P(),
        P(),
    )
    return jax.shard_map(
        local,
        mesh=mesh,
        in_specs=placed,
        out_specs=(
            P("fsdp", None),
            P("fsdp", "rep"),
            P("rep", "fsdp", None, None),
            P("rep", "fsdp", None, None),
        ),
        check_vma=False,
    )
```

```python
import functools

import jax
import jax.numpy as jnp
from jax import lax
from jax.experimental import pallas as pl
from jax.experimental.pallas import tpu as pltpu
from jax.sharding import PartitionSpec as P

NEWTON = 3


BETA_FACTOR = 0.9
BETA_MOMENT = 0.95
EPS_ADAM = 1e-08
EPS_NORM = 1e-06


def move_blocks(steps, source, target, order_ref, in_ref, out_ref, held, in_sem, out_sem):
    def arrive(i):
        return pltpu.make_async_copy(source(i, order_ref, in_ref), held.at[i], in_sem.at[i])

    def leave(i):
        return pltpu.make_async_copy(held.at[i], target(i, order_ref, out_ref), out_sem.at[i])

    def pass_on(i):
        arrive(i).wait()
        leave(i).start()

    pl.loop(0, steps)(lambda i: arrive(i).start())
    pl.loop(0, steps)(pass_on)
    pl.loop(0, steps)(lambda i: leave(i).wait())


def move_call(steps, source, target, order, array, held_shape, out_shape, name):
    return pl.pallas_call(
        functools.partial(move_blocks, steps, source, target),
        in_specs=[pl.BlockSpec(memory_space=pltpu.SMEM), pl.BlockSpec(memory_space=pl.ANY)],
        out_specs=pl.BlockSpec(memory_space=pl.ANY),
        out_shape=jax.ShapeDtypeStruct(out_shape, array.dtype),
        scratch_shapes=[
            pltpu.VMEM((steps,) + held_shape, array.dtype),
            pltpu.SemaphoreType.DMA((steps,)),
            pltpu.SemaphoreType.DMA((steps,)),
        ],
        compiler_params=pltpu.CompilerParams(vmem_limit_bytes=16 << 20),
        name=name,
    )(order, array)


def owner_order(rows, order, groups, per_group, pairs, sub_rows, block_size):
    def source(i, order_ref, in_ref):
        pair, group = i // groups, i % groups
        band, slot = pair // per_group, pair % per_group
        col = order_ref[band * groups * per_group + group * per_group + slot]
        return in_ref.at[
            pl.ds(pl.multiple_of(band * sub_rows, sub_rows), sub_rows),
            pl.ds(pl.multiple_of(col * block_size, block_size), block_size),
        ]

    def target(i, order_ref, out_ref):
        return out_ref.at[i // groups, i % groups]

    shape = (sub_rows, block_size)
    return move_call(
        pairs * groups, source, target, order, rows, shape, (pairs, groups) + shape, "owner_order"
    )


def natural_order(pieces, order, groups, per_group, pairs, sub_rows, block_size):
    half = block_size // 2

    def source(i, order_ref, in_ref):
        return in_ref.at[i // (2 * pairs), (i // 2) % pairs, i % 2]

    def target(i, order_ref, out_ref):
        group, pair, side = i // (2 * pairs), (i // 2) % pairs, i % 2
        band, slot = pair // per_group, pair % per_group
        col = order_ref[band * groups * per_group + group * per_group + slot]
        return out_ref.at[
            pl.ds(pl.multiple_of(band * sub_rows, sub_rows), sub_rows),
            pl.ds(pl.multiple_of(col * block_size + side * half, half), half),
        ]

    out_shape = (pairs // per_group * sub_rows, groups * per_group * block_size)
    return move_call(
        groups * pairs * 2, source, target, order, pieces, (sub_rows, half), out_shape, "natural_order"
    )


def exchange_kernel(
    groups, count, per_group, grads_hbm, moments_hbm, root_hbm, factor_hbm,
    upd, moments_out, factor_out, root_out,
    gp, right_buf, left_buf, pieces, block, moments, roots, product, upd_half, adam_out, adam_in,
    square_sums, factor, newton, norm,
    gp_sem, mom_sem, mom_out_sem, root_sem, factor_sem, factor_out_sem, root_out_sem, own_sem,
    right_send, right_recv, left_send, left_recv,
    piece_send, piece_recv, adam_send, adam_recv, root_send, root_recv, sq_send, sq_recv,
    upd_send, upd_recv, ag_right, ag_left, ag_recv,
):
    z, me = lax.axis_index("rep"), lax.axis_index("fsdp")
    pairs, _, sub_rows, size = gp.shape
    half = size // 2
    side, my_pair = me % 2, me // 2
    partner = me + 1 - 2 * side
    last = groups - 1

    def remote(src, dst, send, recv, **where):
        return pltpu.make_async_remote_copy(
            src_ref=src, dst_ref=dst, send_sem=send, recv_sem=recv,
            device_id=where, device_id_type=pl.DeviceIdType.MESH,
        )

    def load(k):
        return pltpu.make_async_copy(grads_hbm.at[k], gp.at[k], gp_sem.at[k])

    load(0).start()
    root_load = pltpu.make_async_copy(root_hbm, roots.at[side], root_sem)
    root_load.start()
    moments_load = pltpu.make_async_copy(moments_hbm, moments, mom_sem)
    moments_load.start()
    factor_load = pltpu.make_async_copy(factor_hbm, factor, factor_sem)
    factor_load.start()
    pl.loop(1, pairs)(lambda k: load(k).start())

    barrier = pltpu.get_barrier_semaphore()

    @pl.loop(1, count)
    def _(offset):
        pl.semaphore_signal(
            barrier, inc=1, device_id={"fsdp": (me + offset) % count},
            device_id_type=pl.DeviceIdType.MESH,
        )

    @pl.when(z > 0)
    def _():
        pl.semaphore_signal(
            barrier, inc=1, device_id={"rep": z - 1}, device_id_type=pl.DeviceIdType.MESH
        )

    @pl.when(z < last)
    def _():
        pl.semaphore_signal(
            barrier, inc=1, device_id={"rep": z + 1}, device_id_type=pl.DeviceIdType.MESH
        )

    pl.semaphore_wait(barrier, count - 1 + jnp.minimum(z, 1) + jnp.minimum(last - z, 1))

    def go_right(src, d, k):
        return remote(
            src, right_buf.at[k, d], right_send.at[k, d], right_recv.at[k, d],
            rep=jnp.minimum(z + 1, last),
        )

    def go_left(src, d, k):
        return remote(
            src, left_buf.at[k, d], left_send.at[k, d], left_recv.at[k, d],
            rep=jnp.maximum(z - 1, 0),
        )

    def send_raw(k):
        load(k).wait()
        for j in range(last):

            @pl.when(z == 0)
            def _():
                go_right(gp.at[k, last - j], last - j, k).start()

            @pl.when(z == last)
            def _():
                go_left(gp.at[k, j], j, k).start()

    def add_into(buf, k, d):
        buf[k, d] = (buf[k, d].astype(jnp.float32) + gp[k, d].astype(jnp.float32)).astype(buf.dtype)

    root_copy = remote(roots.at[side], roots.at[side], root_send, root_recv, fsdp=partner)

    def piece_copy(k, t):
        return remote(
            pieces.at[k], block.at[pl.ds(pl.multiple_of(me * sub_rows, sub_rows), sub_rows)],
            piece_send.at[k, t], piece_recv.at[me], fsdp=2 * k + t,
        )

    def adam_copy(k, t):
        return remote(
            adam_out.at[k], adam_in.at[me], adam_send.at[k, t], adam_recv.at[me], fsdp=2 * k + t
        )

    def reduce_slot(k):
        for j in range(last):
            far, near = last - j, j

            @pl.when((z > 0) & (z < far))
            def _():
                go_right(right_buf.at[k, far], far, k).wait_recv()
                add_into(right_buf, k, far)
                go_right(right_buf.at[k, far], far, k).start()

            @pl.when((z < last) & (z > near))
            def _():
                go_left(left_buf.at[k, near], near, k).wait_recv()
                add_into(left_buf, k, near)
                go_left(left_buf.at[k, near], near, k).start()

        @pl.when(z > 0)
        def _():
            go_right(right_buf.at[k, z], z, k).wait_recv()

        @pl.when(z < last)
        def _():
            go_left(left_buf.at[k, z], z, k).wait_recv()

        @pl.when(k == 0)
        def _():
            moments_load.wait()

        band, slot = k // per_group, k % per_group
        cols = pl.ds(pl.multiple_of(slot * size, size), size)

        def rows_step(i, total):
            part = pl.ds(pl.multiple_of(i * 16, 16), 16)
            rows = pl.ds(pl.multiple_of(band * sub_rows + i * 16, 16), 16)
            own = gp[k, z, part, :].astype(jnp.float32)
            from_left = right_buf[k, z, part, :].astype(jnp.float32)
            from_right = left_buf[k, z, part, :].astype(jnp.float32)
            own = own + jnp.where(z > 0, from_left, 0.0) + jnp.where(z < last, from_right, 0.0)
            gradient = own / groups
            moment = BETA_MOMENT * moments[rows, cols] + (1.0 - BETA_MOMENT) * gradient * gradient
            moments[rows, cols] = moment
            pieces[k, part, :] = gradient.astype(jnp.bfloat16)
            step = gradient / (jnp.sqrt(moment) + EPS_ADAM)
            return total + step * step

        total = lax.fori_loop(
            0, sub_rows // 16, rows_step, jnp.zeros((16, size), jnp.float32), unroll=2
        )
        adam_out[k] = jnp.full((8, 128), jnp.sum(total), jnp.float32)
        for t in range(2):

            @pl.when(me != 2 * k + t)
            def _():
                piece_copy(k, t).start()
                adam_copy(k, t).start()

        @pl.when(my_pair == k)
        def _():
            block[pl.ds(pl.multiple_of(me * sub_rows, sub_rows), sub_rows), :] = pieces[k]
            adam_in[me] = adam_out[k]

    tile = 256

    def own_slot(k):
        @pl.loop(0, count)
        def _(f):
            @pl.when(f != me)
            def _():
                remote(
                    pieces.at[k], block.at[pl.ds(pl.multiple_of(f * sub_rows, sub_rows), sub_rows)],
                    piece_send.at[k, 0], piece_recv.at[f], fsdp=partner,
                ).wait_recv()
                remote(
                    adam_out.at[k], adam_in.at[f], adam_send.at[k, 0], adam_recv.at[f], fsdp=partner
                ).wait_recv()

        root_copy_in = remote(
            roots.at[1 - side], roots.at[1 - side], root_send, root_recv, fsdp=partner
        )
        root_copy_in.wait_recv()
        half_cols = pl.ds(pl.multiple_of(side * half, half), half)

        def multiply(i, total):
            rows = pl.ds(pl.multiple_of(i * tile, tile), tile)
            mixed = jnp.dot(
                roots[0, rows, :], block[...], preferred_element_type=jnp.float32
            ).astype(jnp.bfloat16)
            result = jnp.dot(mixed, roots[1, :, half_cols], preferred_element_type=jnp.float32)
            product[rows, :] = result
            return total + jnp.sum(result * result)

        total = lax.fori_loop(0, size // tile, multiply, jnp.float32(0.0))
        square_sums[side] = jnp.full((8, 128), total, jnp.float32)
        remote(square_sums.at[side], square_sums.at[side], sq_send, sq_recv, fsdp=partner).start()
        remote(
            square_sums.at[1 - side], square_sums.at[1 - side], sq_send, sq_recv, fsdp=partner
        ).wait_recv()
        product_sq = square_sums[0] + square_sums[1]
        adam_sq = jnp.sum(adam_in[...], axis=0)
        scale = (jnp.sqrt(adam_sq) * lax.rsqrt(product_sq + EPS_NORM))[:1, :1]

        @pl.loop(0, count)
        def _(step):
            f = (me + step) % count
            rows = pl.ds(pl.multiple_of(f * sub_rows, sub_rows), sub_rows)
            upd_half[rows, :] = (product[rows, :] * scale).astype(jnp.bfloat16)

            @pl.when(f != me)
            def _():
                remote(
                    upd_half.at[rows], upd.at[z, k, side], upd_send.at[f], upd_recv.at[k, side],
                    fsdp=f,
                ).start()

            @pl.when(f == me)
            def _():
                pltpu.make_async_copy(upd_half.at[rows], upd.at[z, k, side], own_sem).start()

    def pass_right(s, k):
        return remote(
            upd.at[s, k], upd.at[s, k], ag_right.at[s, k], ag_recv.at[s, k],
            rep=jnp.minimum(z + 1, last),
        )

    def pass_left(s, k):
        return remote(
            upd.at[s, k], upd.at[s, k], ag_left.at[s, k], ag_recv.at[s, k],
            rep=jnp.maximum(z - 1, 0),
        )

    def tiles(body):
        pl.loop(0, size // tile)(lambda i: body(pl.ds(pl.multiple_of(i * tile, tile), tile)))

    def times(dst, lhs, rhs):
        @tiles
        def _(rows):
            newton[dst, rows, :] = jnp.dot(
                newton[lhs, rows, :], newton[rhs], preferred_element_type=jnp.float32
            ).astype(jnp.bfloat16)

    def step_rows(rows, state):
        shape = (tile, size)
        on_diagonal = lax.broadcasted_iota(jnp.int32, shape, 0) + rows.start == (
            lax.broadcasted_iota(jnp.int32, shape, 1)
        )
        return ((jnp.where(on_diagonal, 5.0, 0.0) - state.astype(jnp.float32)) * 0.25).astype(
            jnp.bfloat16
        )

    def step_from(state):
        @tiles
        def _(rows):
            newton[1, rows, :] = step_rows(rows, newton[state, rows, :])

    def gram():
        factor_load.wait()

        @pl.when(side == 0)
        def _():
            @tiles
            def _(rows):
                newton[3, rows, :] = block[rows, :]

        @pl.when(side == 1)
        def _():
            @tiles
            def _(rows):
                newton[3, :, rows] = block[rows, :].T

        def add_gram(i, total):
            rows = pl.ds(pl.multiple_of(i * tile, tile), tile)
            product_rows = lax.dot_general(
                newton[3, rows, :], newton[3], (((1,), (1,)), ((), ())),
                preferred_element_type=jnp.float32,
            )
            new = BETA_FACTOR * factor[rows, :] + (1.0 - BETA_FACTOR) * product_rows
            factor[rows, :] = new
            return total + jnp.sum(new * new)

        total = lax.fori_loop(0, size // tile, add_gram, jnp.float32(0.0))
        norm[...] = jnp.sqrt(jnp.full((8, 128), total, jnp.float32))
        pltpu.make_async_copy(factor, factor_out, factor_out_sem).start()

    def seed():
        z_norm = norm[...]
        first = lax.rsqrt(jnp.sqrt(z_norm))[:1, :1].astype(jnp.bfloat16).astype(jnp.float32)

        @tiles
        def _(rows):
            state = (factor[rows, :] / z_norm[:1, :1]).astype(jnp.bfloat16)
            newton[0, rows, :] = state
            step_mat = step_rows(rows, state)
            newton[1, rows, :] = step_mat
            newton[4, rows, :] = (first * step_mat.astype(jnp.float32)).astype(jnp.bfloat16)

    def first_state():
        times(2, 3, 0)
        step_from(2)

    def second_state():
        times(3, 4, 2)
        step_from(3)

    def finish():
        times(2, 0, 1)
        pltpu.make_async_copy(newton.at[2], root_out, root_out_sem).start()

    stages = [
        gram, seed, lambda: times(2, 1, 1), lambda: times(3, 2, 2), first_state,
        lambda: times(0, 4, 1), lambda: times(3, 1, 1), lambda: times(4, 3, 3), second_state,
        finish,
    ]

    def gather_start(k):
        for t in range(2):

            @pl.when(me == 2 * k + t)
            def _():
                pltpu.make_async_copy(
                    upd_half.at[pl.ds(pl.multiple_of(me * sub_rows, sub_rows), sub_rows)],
                    upd.at[z, k, t], own_sem,
                ).wait()

            @pl.when(me != 2 * k + t)
            def _():
                remote(
                    upd_half.at[pl.ds(0, sub_rows)], upd.at[z, k, t], upd_send.at[0],
                    upd_recv.at[k, t], fsdp=partner,
                ).wait_recv()

        @pl.when(z < last)
        def _():
            pass_right(z, k).start()

        @pl.when(z > 0)
        def _():
            pass_left(z, k).start()

    def gather_hop(k, j):
        @pl.when(z - j >= 0)
        def _():
            s = z - j
            pass_right(s, k).wait_recv()

            @pl.when(z < last)
            def _():
                pass_right(s, k).start()

        @pl.when(z + j <= last)
        def _():
            s = z + j
            pass_left(s, k).wait_recv()

            @pl.when(z > 0)
            def _():
                pass_left(s, k).start()

    send_raw(0)
    root_load.wait()
    root_copy.start()
    send_raw(1)

    @pl.loop(0, pairs)
    def _(t):
        @pl.when(t + 2 < pairs)
        def _():
            send_raw(t + 2)

        reduce_slot(t)

        @pl.when(my_pair == t - 1)
        def _():
            own_slot(t - 1)

        @pl.when(t >= 2)
        def _():
            gather_start(t - 2)

        for j in range(1, groups):

            @pl.when(t >= 2 + j)
            def _():
                gather_hop(t - 2 - j, j)

    pltpu.make_async_copy(moments, moments_out, mom_out_sem).start()

    @pl.when(my_pair == pairs - 1)
    def _():
        own_slot(pairs - 1)

    def hops(turn):
        for j in range(groups - 1, 0, -1):
            if 0 <= turn - j < pairs:
                gather_hop(turn - j, j)

    gather_start(pairs - 2)
    hops(pairs - 2)
    gather_start(pairs - 1)
    stages[0]()
    hops(pairs - 1)
    stages[1]()
    for turn in range(groups - 1):
        done = turn + 2
        for stage in stages[done:done + 1] if turn < groups - 2 else stages[done:]:
            stage()
        hops(pairs + turn)
    root_copy.wait_send()
    remote(square_sums.at[side], square_sums.at[side], sq_send, sq_recv, fsdp=partner).wait_send()
    pltpu.make_async_copy(moments, moments_out, mom_out_sem).wait()
    pltpu.make_async_copy(factor, factor_out, factor_out_sem).wait()
    pltpu.make_async_copy(newton.at[2], root_out, root_out_sem).wait()

    @pl.loop(0, count)
    def _(f):
        @pl.when(f != me)
        def _():
            rows = pl.ds(pl.multiple_of(f * sub_rows, sub_rows), sub_rows)
            remote(
                upd_half.at[rows], upd.at[z, my_pair, side], upd_send.at[f],
                upd_recv.at[my_pair, side], fsdp=f,
            ).wait_send()

    @pl.loop(0, pairs)
    def _(k):
        for t in range(2):

            @pl.when(me != 2 * k + t)
            def _():
                piece_copy(k, t).wait_send()
                adam_copy(k, t).wait_send()

        for d in range(groups):

            @pl.when(z < d)
            def _():
                go_right(right_buf.at[k, d], d, k).wait_send()

            @pl.when(z > d)
            def _():
                go_left(left_buf.at[k, d], d, k).wait_send()

            @pl.when((d <= z) & (z < last))
            def _():
                pass_right(d, k).wait_send()

            @pl.when((d >= z) & (z > 0))
            def _():
                pass_left(d, k).wait_send()


def exchange(ordered, moments, root, factor, per_group, count):
    pairs, groups, sub_rows, size = ordered.shape
    half = size // 2
    low, wide = jnp.bfloat16, jnp.float32
    dma = pltpu.SemaphoreType.DMA
    anywhere = pl.BlockSpec(memory_space=pl.ANY)
    return pl.pallas_call(
        functools.partial(exchange_kernel, groups, count, per_group),
        in_specs=[anywhere] * 4,
        out_specs=[anywhere] * 4,
        out_shape=[
            jax.ShapeDtypeStruct((groups, pairs, 2, sub_rows, half), low),
            jax.ShapeDtypeStruct(moments.shape, wide),
            jax.ShapeDtypeStruct((size, size), wide),
            jax.ShapeDtypeStruct((size, size), low),
        ],
        scratch_shapes=[
            pltpu.VMEM((pairs, groups, sub_rows, size), low),
            pltpu.VMEM((pairs, groups, sub_rows, size), low),
            pltpu.VMEM((pairs, groups, sub_rows, size), low),
            pltpu.VMEM((pairs, sub_rows, size), low),
            pltpu.VMEM((size, size), low),
            pltpu.VMEM(moments.shape, wide),
            pltpu.VMEM((2, size, size), low),
            pltpu.VMEM((size, half), wide),
            pltpu.VMEM((size, half), low),
            pltpu.VMEM((pairs, 8, 128), wide),
            pltpu.VMEM((count, 8, 128), wide),
            pltpu.VMEM((2, 8, 128), wide),
            pltpu.VMEM((size, size), wide),
            pltpu.VMEM((5, size, size), low),
            pltpu.VMEM((8, 128), wide),
            dma((pairs,)), dma, dma, dma, dma, dma, dma, dma,
            dma((pairs, groups)), dma((pairs, groups)), dma((pairs, groups)), dma((pairs, groups)),
            dma((pairs, 2)), dma((count,)), dma((pairs, 2)), dma((count,)), dma, dma, dma, dma,
            dma((count,)), dma((pairs, 2)), dma((groups, pairs)), dma((groups, pairs)),
            dma((groups, pairs)),
        ],
        compiler_params=pltpu.CompilerParams(
            collective_id=0, has_side_effects=True, vmem_limit_bytes=56 << 20
        ),
        name="exchange",
    )(ordered, moments, root, factor)


def local(grads, moments, factors, roots, refresh, owner):
    block_size = factors.shape[2]
    height = grads.shape[1]
    width_all = grads.shape[2]
    band_span = block_size // height
    groups = lax.axis_size("rep")
    columns = width_all // block_size
    per_group = columns // groups
    fsdp_count = lax.axis_size("fsdp")
    sub_rows = block_size // fsdp_count
    band_count = height // sub_rows
    half_cols = block_size // 2
    group_index = lax.axis_index("rep")
    fsdp_index = lax.axis_index("fsdp")
    band_index = fsdp_index // band_span
    local_index = fsdp_index % band_span
    side_index = local_index % 2
    slot_index = local_index // 2
    col_range = jnp.arange(columns, dtype=jnp.int32)
    col_order = jnp.argsort(owner * columns + col_range[None, :], axis=1)
    pairs = band_count * per_group
    order = col_order.reshape(-1).astype(jnp.int32)
    ordered = owner_order(grads[0], order, groups, per_group, pairs, sub_rows, block_size)
    own_root = roots[0, 0]
    gathered, new_moments, new_factor, fresh_root = exchange(
        ordered, moments, own_root, factors[0, 0], per_group, fsdp_count
    )
    update = natural_order(gathered, order, groups, per_group, pairs, sub_rows, block_size)
    pair_ids = refresh // 2
    listed_band = pair_ids // columns
    listed_col = pair_ids % columns
    listed_rows = jnp.take(owner, listed_band, axis=0)
    listed_group = jnp.take_along_axis(listed_rows, listed_col[:, None], axis=1)[:, 0]
    listed_rank = jnp.sum(
        (
            (listed_rows == listed_group[:, None]) & (col_range[None, :] < listed_col[:, None])
        ).astype(jnp.int32),
        axis=1,
    )
    listed_fsdp = listed_band * band_span + 2 * listed_rank + refresh % 2
    chosen = jnp.any((listed_group == group_index) & (listed_fsdp == fsdp_index))
    new_root = jnp.where(chosen, fresh_root, own_root)
    return (update, new_moments, new_factor[None, None], new_root[None, None])


def solution(mesh):
    placed = (
        P("rep", "fsdp", None),
        P("fsdp", "rep"),
        P("rep", "fsdp", None, None),
        P("rep", "fsdp", None, None),
        P(),
        P(),
    )
    return jax.shard_map(
        local,
        mesh=mesh,
        in_specs=placed,
        out_specs=(
            P("fsdp", None),
            P("fsdp", "rep"),
            P("rep", "fsdp", None, None),
            P("rep", "fsdp", None, None),
        ),
        check_vma=False,
    )
```
